256 devices in a mesh: grp: 8 (over z), shard: 32 (over y, x, core).
Axes of the slice: x: 4, y: 4, z: 8, core: 2. Of those that a mesh axis runs over, the one named last changes fastest.
Arguments:
- activations: bfloat16 [32768, 8192], P('grp', 'shard'), may hold values from -6 to 6
- cotangent: bfloat16 [32768, 28672], P('grp', 'shard'), may hold values from -0.29882812 to 0.29882812
- adapter_down_matrices: bfloat16 [64, 16, 8192], P('grp', None, 'shard'), may hold values from -0.0625 to 0.0625
- adapter_up_weight: bfloat16 [64, 16, 28672], P('grp', None, 'shard'), may hold values from -0.03125 to 0.03125
- down_feedback_residual: float32 [64, 16, 8192], P('grp', None, 'shard'), may hold values from -3 to 3
- up_feedback_residual: float32 [64, 16, 28672], P('grp', None, 'shard'), may hold values from -3 to 3
- group_tenant_adapters: int32 [8, 8], replicated, may hold values from 0 to 63, as said below
- adapter_owner_slot: int32 [64], replicated, may hold values from 0 to 63, as said below
- block_list_entry: int32 [128], P('grp'), may hold values from 0 to 7
- block_token_rows: int32 [128], P('grp'), may hold values from 1 to 256, as said below
Outputs:
- grad_down: float32 [64, 16, 8192], P('grp', None, 'shard')
- grad_up: float32 [64, 16, 28672], P('grp', None, 'shard')
The draws below stay inside these ranges and needn't reach their ends.
Inputs may be any that keep to these rules, and one draw needn't show every extreme that they name: adapter_owner_slot is a permutation. `group_tenant_adapters`: each row names 8 different adapters; at most 2 entries of a row lie with one owner group, and one owner group holds exactly 2 entries of every row. `block_token_rows`: some block of every draw is full.
All inputs are finite; a program needn't handle non-finite values.
Results may differ from the reference program's by a relative error of at most 0.0028.
Values may be sent and summed in bfloat16 or wider, within the bound.
A program may use at most 64 MiB of HBM per device.

```python
import jax
import jax.numpy as jnp
from jax import lax

MODEL_WIDTH = 8192
HIDDEN_UNITS = 28672
ADAPTER_RANK = 16
ADAPTER_COUNT = 64
LISTED = 8
CAP = 2
BLK = 256
BLOCKS = 16
ROWS = 4096
TOKENS = 32768
N_GRP = 8


def tenancy(key):
    slot_of = jax.random.permutation(jax.random.fold_in(key, 11), ADAPTER_COUNT).astype(jnp.int32)
    adapter_of = jnp.argsort(slot_of, stable=True).astype(jnp.int32)
    slots_per_owner = ADAPTER_COUNT // N_GRP
    favored = jax.random.randint(jax.random.fold_in(key, 12), (), 0, N_GRP)

    def one_row(row_random_key):
        spread_idx = jax.random.permutation(jax.random.fold_in(row_random_key, 1), slots_per_owner)
        favored_idx = jax.random.permutation(jax.random.fold_in(row_random_key, 2), slots_per_owner)
        others = jnp.arange(LISTED - CAP, dtype=jnp.int32)
        other_owner = (favored + 1 + others % (N_GRP - 1)) % N_GRP
        other_slots = other_owner * slots_per_owner + spread_idx[:LISTED - CAP]
        favored_slots = favored * slots_per_owner + favored_idx[:CAP]
        row_slots = jnp.concatenate([favored_slots, other_slots]).astype(jnp.int32)
        order = jax.random.permutation(jax.random.fold_in(row_random_key, 3), LISTED)
        return jnp.take(adapter_of, jnp.take(row_slots, order))
    row_keys = jax.random.split(jax.random.fold_in(key, 13), N_GRP)
    lists = jax.vmap(one_row)(row_keys)
    return (slot_of, lists.astype(jnp.int32))


def draw_group_tenant_adapters(key, part):
    slot_of, lists = tenancy(key)
    return lists


def draw_adapter_owner_slot(key, part):
    slot_of, lists = tenancy(key)
    return slot_of


def draw_block_token_rows(key, part):
    key = jax.random.fold_in(key, 3)
    total = N_GRP * BLOCKS
    short = jax.random.randint(jax.random.fold_in(key, 1), (total,), 1, BLK + 1)
    full = jax.random.randint(jax.random.fold_in(key, 2), (total,), 0, 2) == 1
    counts = jnp.where(full, BLK, short).astype(jnp.int32)
    return counts.at[0].set(BLK)


def with_ends(array, own_key, low, high):
    longest = array.shape.index(max(array.shape))
    spots = []
    for shift in (0, 1):
        where = [jax.random.randint(jax.random.fold_in(own_key, axis), (), 0, length) for axis, length in enumerate(array.shape)]
        where[longest] = (where[longest] + shift) % array.shape[longest]
        spots.append(tuple(where))
    return array.at[spots[0]].set(low).at[spots[1]].set(high)


def level_of(key, dims, shards, smallest, largest):
    factor_of, own = 1.0, jax.random.fold_in(key, 6)
    for position, shards_of in shards:
        draws = jnp.exp(jax.random.uniform(jax.random.fold_in(own, position), (shards_of,), jnp.float32, smallest / len(shards), largest / len(shards)))
        factor_of = factor_of * jnp.repeat(draws, dims[position] // shards_of).reshape([-1 if axis == position else 1 for axis in range(len(dims))])
    return factor_of


def gaussian(key, extent, spread, reach, pieces=(), kind=jnp.bfloat16):
    level = level_of(key, extent, pieces, -0.22, 0.18) if pieces else 1.0
    array = jax.random.normal(key, extent, jnp.float32) * spread * level
    return jnp.minimum(jnp.maximum(array, -reach), reach).astype(kind)


def setup_inputs(seed: int = 0) -> dict:
    key_list = jax.random.split(jax.random.key(seed), 11)
    return {
        "activations": gaussian(key_list[0], (TOKENS, MODEL_WIDTH), 1.0, 6.0, ((0, 8), (1, 32))),
        "cotangent": gaussian(key_list[1], (TOKENS, HIDDEN_UNITS), 0.05, 0.29882812, ((0, 8), (1, 32))),
        "adapter_down_matrices": gaussian(key_list[2], (ADAPTER_COUNT, ADAPTER_RANK, MODEL_WIDTH), MODEL_WIDTH ** -0.5, 0.0625, ((0, 8), (2, 32))),
        "adapter_up_weight": gaussian(key_list[3], (ADAPTER_COUNT, ADAPTER_RANK, HIDDEN_UNITS), HIDDEN_UNITS ** -0.5, 0.03125, ((0, 8), (2, 32))),
        "down_feedback_residual": gaussian(key_list[4], (N_GRP * LISTED, ADAPTER_RANK, MODEL_WIDTH), 0.5, 3.0, ((0, 8), (2, 32)), jnp.float32),
        "up_feedback_residual": gaussian(key_list[5], (N_GRP * LISTED, ADAPTER_RANK, HIDDEN_UNITS), 0.5, 3.0, ((0, 8), (2, 32)), jnp.float32),
        "group_tenant_adapters": draw_group_tenant_adapters(jax.random.fold_in(key_list[10], 71), 0),
        "adapter_owner_slot": draw_adapter_owner_slot(jax.random.fold_in(key_list[10], 71), 0),
        "block_list_entry": with_ends(jax.random.randint(key_list[8], (N_GRP * BLOCKS,), 0, LISTED), jax.random.fold_in(key_list[8], 1), 0, LISTED - 1).astype(jnp.int32),
        "block_token_rows": draw_block_token_rows(jax.random.fold_in(key_list[10], 71), 0),
    }


adapter_scale = 2.0


def listed_slots(group_tenant_adapters, adapter_owner_slot):
    match = group_tenant_adapters[:, :, None] == jnp.arange(ADAPTER_COUNT, dtype=jnp.int32)[None, None, :]
    return jnp.sum(jnp.where(match, adapter_owner_slot[None, None, :], 0), axis=2).astype(jnp.int32)


def reference(activations, cotangent, adapter_down_matrices, adapter_up_weight, down_feedback_residual, up_feedback_residual, group_tenant_adapters, adapter_owner_slot, block_list_entry, block_token_rows):
    slots = listed_slots(group_tenant_adapters, adapter_owner_slot)
    highest_precision = lax.Precision.HIGHEST

    def one_group(group):
        input_token_rows = lax.dynamic_slice_in_dim(activations, group * ROWS, ROWS, 0).astype(jnp.float32).reshape(BLOCKS, BLK, MODEL_WIDTH)
        upstream = lax.dynamic_slice_in_dim(cotangent, group * ROWS, ROWS, 0).astype(jnp.float32).reshape(BLOCKS, BLK, HIDDEN_UNITS)
        own_slots = lax.dynamic_index_in_dim(slots, group, 0, keepdims=False)
        entries = lax.dynamic_slice_in_dim(block_list_entry, group * BLOCKS, BLOCKS, 0)
        counts = lax.dynamic_slice_in_dim(block_token_rows, group * BLOCKS, BLOCKS, 0)
        block_owner_slots = jnp.take(own_slots, entries, axis=0).astype(jnp.int32)
        down_block_gradients = jnp.take(adapter_down_matrices, block_owner_slots, axis=0).astype(jnp.float32)
        up_block_grads = jnp.take(adapter_up_weight, block_owner_slots, axis=0).astype(jnp.float32)
        rank_input = jnp.einsum("ily,iuy->ilu", down_block_gradients, input_token_rows, precision=highest_precision)
        low_back = jnp.einsum("brf,bkf->brk", up_block_grads, upstream, precision=highest_precision)
        valid_token_mask = (jnp.arange(BLK, dtype=jnp.int32)[None, :] < counts[:, None]).astype(jnp.float32)
        frozen_weight = adapter_scale * valid_token_mask[:, None, :]
        scaled_in = lax.optimization_barrier((rank_input * frozen_weight).astype(jnp.bfloat16)).astype(jnp.float32)
        scaled_backward = lax.optimization_barrier((low_back * frozen_weight).astype(jnp.bfloat16)).astype(jnp.float32)
        block_up = jnp.einsum("brk,bkf->brf", scaled_in, upstream, precision=highest_precision)
        block_down_gradient = jnp.einsum("sli,sit->slt", scaled_backward, input_token_rows, precision=highest_precision)
        onehot = (entries[:, None] == jnp.arange(LISTED, dtype=jnp.int32)[None, :]).astype(jnp.float32)
        step_up = jnp.einsum("be,brf->erf", onehot, block_up, precision=highest_precision)
        step_down = jnp.einsum("be,brd->erd", onehot, block_down_gradient, precision=highest_precision)
        held_down = lax.dynamic_slice_in_dim(down_feedback_residual, group * LISTED, LISTED, 0)
        held_up = lax.dynamic_slice_in_dim(up_feedback_residual, group * LISTED, LISTED, 0)
        return step_down + held_down, step_up + held_up

    sent_down, sent_up = lax.map(one_group, jnp.arange(N_GRP, dtype=jnp.int32))
    flat = slots.reshape(N_GRP * LISTED)
    grad_down = jnp.zeros((ADAPTER_COUNT, ADAPTER_RANK, MODEL_WIDTH), jnp.float32).at[flat].add(sent_down.reshape(N_GRP * LISTED, ADAPTER_RANK, MODEL_WIDTH))
    grad_up = jnp.zeros((ADAPTER_COUNT, ADAPTER_RANK, HIDDEN_UNITS), jnp.float32).at[flat].add(sent_up.reshape(N_GRP * LISTED, ADAPTER_RANK, HIDDEN_UNITS))
    return grad_down, grad_up
```

```python
import functools

import jax
import jax.numpy as jnp
from jax import lax
from jax.experimental import pallas as pl
from jax.experimental.pallas import tpu as pltpu
from jax.sharding import PartitionSpec as P

MESH = pl.DeviceIdType.MESH
bf16, f32, i32 = jnp.bfloat16, jnp.float32, jnp.int32
adapter_scale = 2.0


def kernel(
    groups,
    shards,
    x_hbm,
    c_hbm,
    ad_hbm,
    au_hbm,
    rd_hbm,
    ru_hbm,
    lists,
    slot_of,
    entry_of,
    rows_of,
    gd_hbm,
    gu_hbm,
    x,
    c,
    ad,
    au,
    rd,
    ru,
    ad_out,
    au_out,
    ad_in,
    au_in,
    part_x,
    part_c,
    rs_x,
    rs_c,
    ag_x,
    ag_c,
    spread,
    acc_d,
    acc_u,
    gd_out,
    gu_out,
    gd_in,
    gu_in,
    gd,
    gu,
    slot_tab,
    entry_tab,
    place_tab,
    load_sem,
    ad_send,
    ad_recv,
    au_send,
    au_recv,
    xy_send,
    xy_recv,
    gd_send,
    gd_recv,
    gu_send,
    gu_recv,
    store_sem,
):
    chips = shards // 2
    per_owner, rank, _ = ad.shape
    listed = rd.shape[0]
    block = x.shape[0] // chips
    half = block // 2
    me = lax.axis_index("grp")
    sh = lax.axis_index("shard")
    chip, core = lax.div(sh, 2), lax.rem(sh, 2)
    order = sorted(range(1, groups), key=lambda d: -min(d, groups - d))

    def group_at(d):
        return lax.rem(me + d, groups)

    loads = [
        pltpu.make_async_copy(src, dst, load_sem.at[i])
        for i, (src, dst) in enumerate(
            ((ad_hbm, ad), (au_hbm, au), (x_hbm, x), (c_hbm, c), (rd_hbm, rd), (ru_hbm, ru))
        )
    ]
    for load in loads:
        load.start()

    barrier = pltpu.get_barrier_semaphore()
    for d in range(1, groups):
        pl.semaphore_signal(barrier, inc=1, device_id=(group_at(d), sh), device_id_type=MESH)

    def greet(d, _):
        pl.semaphore_signal(
            barrier, inc=1, device_id=(me, lax.rem(sh + d, shards)), device_id_type=MESH
        )
        return _

    lax.fori_loop(1, shards, greet, 0)

    firsts = []
    for d in range(groups):
        row = group_at(d)
        first, second = i32(-1), i32(-1)
        for e in range(listed):
            s = slot_of[lists[row, e]]
            mine = lax.div(s, i32(per_owner)) == me
            at = lax.rem(s, i32(per_owner))
            second = jnp.where(mine & (first >= 0), at, second)
            first = jnp.where(mine & (first < 0), at, first)
        slot_tab[2 * d] = first
        slot_tab[2 * d + 1] = second
        firsts.append((jnp.maximum(first, 0), jnp.maximum(second, 0)))

    loads[0].wait()
    loads[1].wait()
    for d in range(groups):
        for k in range(2):
            if d:
                ad_out[d - 1, k] = ad[firsts[d][k]]
                au_out[d - 1, k] = au[firsts[d][k]]
            else:
                ad_in[2 * me + k] = ad[firsts[d][k]]
                au_in[2 * me + k] = au[firsts[d][k]]

    pl.semaphore_wait(barrier, groups - 1 + shards - 1)

    for out, into, send, recv in ((ad_out, ad_in, ad_send, ad_recv), (au_out, au_in, au_send, au_recv)):
        for d in order:
            pltpu.make_async_remote_copy(
                src_ref=out.at[d - 1],
                dst_ref=into.at[pl.ds(2 * me, 2)],
                send_sem=send,
                recv_sem=recv,
                device_id=(group_at(d), sh),
                device_id_type=MESH,
            ).start()

    owners = []
    for e in range(listed):
        owners.append(lax.div(slot_of[lists[me, e]], i32(per_owner)))
    places = []
    for e in range(listed):
        k = i32(0)
        for before in range(e):
            k = k + jnp.where(owners[before] == owners[e], 1, 0)
        places.append(2 * owners[e] + k)
        place_tab[e] = places[e]
    for p in range(2 * groups):
        found = i32(0)
        for e in range(listed):
            found = jnp.where(places[e] == p, e, found)
        entry_tab[p] = found

    def all_bytes(ref, sem):
        pltpu.make_async_copy(ref, ref, sem).wait()

    def low_rank(tokens, adapters, part, rs, ag, which):
        send, recv = xy_send.at[2 * which], xy_recv.at[2 * which]

        def project(i):
            b = lax.rem(chip + i, chips)
            low = lax.dot_general(
                adapters[place_tab[entry_of[b]]],
                tokens[pl.ds(pl.multiple_of(b * block, block), block), :],
                (((1,), (1,)), ((), ())),
                preferred_element_type=f32,
            )
            part[b, 0] = low[:, :half]
            part[b, 1] = low[:, half:]
            return b

        def send_part(b, k, slot):
            pltpu.make_async_remote_copy(
                src_ref=part.at[b, k],
                dst_ref=rs.at[slot],
                send_sem=send,
                recv_sem=recv,
                device_id=(me, 2 * b + k),
                device_id_type=MESH,
            ).start()

        step = 3 if (chips - 1) % 3 == 0 else 1

        def some(j, _):
            first = 1 + j * step
            at = [project(first + t) for t in range(step)]
            for t in range(step):
                for k in range(2):
                    send_part(at[t], k, 2 * (first + t - 1) + core)
            return _

        lax.fori_loop(0, (chips - 1) // step, some, 0)
        project(0)
        send_part(chip, 1 - core, shards - 2)
        all_bytes(rs, recv)

        low = part[chip, core] + jnp.sum(rs[...], axis=0)
        token = core * half + lax.broadcasted_iota(i32, (rank, half), 1)
        scale = jnp.where(token < rows_of[chip], adapter_scale, 0.0)
        ag[sh] = (low * scale).astype(bf16)

        send, recv = xy_send.at[2 * which + 1], xy_recv.at[2 * which + 1]

        def give(b, k):
            pltpu.make_async_remote_copy(
                src_ref=ag.at[sh],
                dst_ref=ag.at[sh],
                send_sem=send,
                recv_sem=recv,
                device_id=(me, 2 * b + k),
                device_id_type=MESH,
            ).start()

        def give_chip(i, _):
            b = lax.rem(chip + i, chips)
            give(b, 0)
            give(b, 1)
            return _

        lax.fori_loop(1, chips, give_chip, 0)
        give(chip, 1 - core)
        all_bytes(ag.at[pl.ds(0, shards - 1)], recv)

    def gradient(ag, tokens, residual, acc):
        def place(b, _):
            e = entry_of[b]
            for h in range(2):
                columns = pl.ds(pl.multiple_of(b * block + h * half, half), half)
                v = ag[2 * b + h]
                for l in range(listed):
                    spread[l * rank : (l + 1) * rank, columns] = jnp.where(e == l, v, jnp.zeros_like(v))
            return _

        lax.fori_loop(0, chips, place, 0)
        width = tokens.shape[1]
        for start in range(0, width, 256):
            stop = min(start + 256, width)
            step = jnp.dot(spread[...], tokens[:, start:stop], preferred_element_type=f32)
            acc[:, :, start:stop] = step.reshape(listed, rank, stop - start) + residual[:, :, start:stop]

    def send_gradient(acc, out, into, send, recv):
        for d in order:
            owner = group_at(d)
            for k in range(2):
                out[d - 1, k] = acc[entry_tab[2 * owner + k]].astype(bf16)
            pltpu.make_async_remote_copy(
                src_ref=out.at[d - 1],
                dst_ref=into.at[d - 1],
                send_sem=send,
                recv_sem=recv.at[d - 1],
                device_id=(owner, sh),
                device_id_type=MESH,
            ).start()

    def collect(acc, into, recv, total):
        values = [acc[entry_tab[2 * me + k]] for k in range(2)]
        for s in range(per_owner):
            total[s] = jnp.where(slot_tab[0] == s, values[0], 0.0) + jnp.where(
                slot_tab[1] == s, values[1], 0.0
            )
        for d in reversed(order):
            all_bytes(into.at[d - 1], recv.at[d - 1])
            values = [into[d - 1, k].astype(f32) for k in range(2)]
            at = [slot_tab[2 * (groups - d) + k] for k in range(2)]
            for s in range(per_owner):
                total[s] += jnp.where(at[0] == s, values[0], 0.0) + jnp.where(
                    at[1] == s, values[1], 0.0
                )

    loads[2].wait()
    all_bytes(ad_in.at[pl.ds(0, 2 * groups - 2)], ad_recv)
    low_rank(x, ad_in, part_x, rs_x, ag_x, 0)
    loads[3].wait()
    loads[5].wait()
    gradient(ag_x, c, ru, acc_u)
    send_gradient(acc_u, gu_out, gu_in, gu_send, gu_recv)

    all_bytes(au_in.at[pl.ds(0, 2 * groups - 2)], au_recv)
    low_rank(c, au_in, part_c, rs_c, ag_c, 1)
    loads[4].wait()
    gradient(ag_c, x, rd, acc_d)
    send_gradient(acc_d, gd_out, gd_in, gd_send, gd_recv)

    collect(acc_u, gu_in, gu_recv, gu)
    store_u = pltpu.make_async_copy(gu, gu_hbm, store_sem.at[0])
    store_u.start()
    collect(acc_d, gd_in, gd_recv, gd)
    store_d = pltpu.make_async_copy(gd, gd_hbm, store_sem.at[1])
    store_d.start()

    all_bytes(ad_out, ad_send)
    all_bytes(au_out, au_send)
    all_bytes(rs_x, xy_send.at[0])
    all_bytes(ag_x.at[pl.ds(0, shards - 1)], xy_send.at[1])
    all_bytes(rs_c, xy_send.at[2])
    all_bytes(ag_c.at[pl.ds(0, shards - 1)], xy_send.at[3])
    all_bytes(gu_out, gu_send)
    all_bytes(gd_out, gd_send)
    store_u.wait()
    store_d.wait()


def solution(mesh):
    groups, shards = mesh.shape["grp"], mesh.shape["shard"]

    def local(x, c, ad, au, rd, ru, lists, slot_of, entry_of, rows_of):
        tokens, wd = x.shape
        wu = c.shape[1]
        per_owner, rank, _ = ad.shape
        listed = lists.shape[1]
        chips = shards // 2
        half = tokens // chips // 2
        vmem, dma = pltpu.VMEM, pltpu.SemaphoreType.DMA
        places = 2 * groups
        return pl.pallas_call(
            functools.partial(kernel, groups, shards),
            out_shape=(
                jax.ShapeDtypeStruct((per_owner, rank, wd), f32),
                jax.ShapeDtypeStruct((per_owner, rank, wu), f32),
            ),
            in_specs=[pl.BlockSpec(memory_space=pltpu.HBM)] * 6
            + [pl.BlockSpec(memory_space=pltpu.SMEM)] * 4,
            out_specs=[pl.BlockSpec(memory_space=pltpu.HBM)] * 2,
            scratch_shapes=[
                vmem((tokens, wd), bf16),
                vmem((tokens, wu), bf16),
                vmem((per_owner, rank, wd), bf16),
                vmem((per_owner, rank, wu), bf16),
                vmem((listed, rank, wd), f32),
                vmem((listed, rank, wu), f32),
                vmem((groups - 1, 2, rank, wd), bf16),
                vmem((groups - 1, 2, rank, wu), bf16),
                vmem((places, rank, wd), bf16),
                vmem((places, rank, wu), bf16),
                vmem((chips, 2, rank, half), f32),
                vmem((chips, 2, rank, half), f32),
                vmem((shards - 1, rank, half), f32),
                vmem((shards - 1, rank, half), f32),
                vmem((shards, rank, half), bf16),
                vmem((shards, rank, half), bf16),
                vmem((listed * rank, tokens), bf16),
                vmem((listed, rank, wd), f32),
                vmem((listed, rank, wu), f32),
                vmem((groups - 1, 2, rank, wd), bf16),
                vmem((groups - 1, 2, rank, wu), bf16),
                vmem((groups - 1, 2, rank, wd), bf16),
                vmem((groups - 1, 2, rank, wu), bf16),
                vmem((per_owner, rank, wd), f32),
                vmem((per_owner, rank, wu), f32),
                pltpu.SMEM((places,), i32),
                pltpu.SMEM((places,), i32),
                pltpu.SMEM((listed,), i32),
                dma((6,)),
                dma,
                dma,
                dma,
                dma,
                dma((4,)),
                dma((4,)),
                dma,
                dma((groups - 1,)),
                dma,
                dma((groups - 1,)),
                dma((2,)),
            ],
            compiler_params=pltpu.CompilerParams(
                collective_id=0, has_side_effects=True, vmem_limit_bytes=56 * 2**20
            ),
        )(x, c, ad, au, rd, ru, lists, slot_of, entry_of, rows_of)

    split = P("grp", None, "shard")
    return jax.shard_map(
        local,
        mesh=mesh,
        in_specs=(P("grp", "shard"),) * 2 + (split,) * 4 + (P(), P(), P("grp"), P("grp")),
        out_specs=(split, split),
        check_vma=False,
    )
```

```python
import functools

import jax
import jax.numpy as jnp
from jax import lax
from jax.experimental import pallas as pl
from jax.experimental.pallas import tpu as pltpu
from jax.sharding import PartitionSpec as P

MESH = pl.DeviceIdType.MESH
bf16, f32, i32 = jnp.bfloat16, jnp.float32, jnp.int32
adapter_scale = 2.0


def grid_of(chips):
    across = 4 if chips % 4 == 0 else chips
    return chips // across, across


def kernel(
    groups,
    shards,
    x_hbm,
    c_hbm,
    ad_hbm,
    au_hbm,
    rd_hbm,
    ru_hbm,
    lists_hbm,
    slot_hbm,
    entry_hbm,
    rows_hbm,
    gd,
    gu,
    x,
    c,
    ad,
    au,
    rd,
    ru,
    ad_out,
    au_out,
    ad_in,
    au_in,
    mine_x,
    mine_c,
    theirs_x,
    theirs_c,
    pair_x,
    pair_c,
    rs_x,
    rs_c,
    ag_x,
    ag_c,
    spread,
    acc_d,
    acc_u,
    gd_out,
    gu_out,
    gd_in,
    gu_in,
    lists,
    slot_of,
    entry_of,
    rows_of,
    slot_tab,
    entry_tab,
    place_tab,
    load_sem,
    table_sem,
    ad_send,
    ad_recv,
    au_send,
    au_recv,
    pair_send,
    pair_recv,
    rs_send,
    rs_recv,
    ag_send,
    ag_recv,
    swap_send,
    swap_recv,
    gd_send,
    gd_recv,
    gu_send,
    gu_recv,
):
    chips = shards // 2
    high, across = grid_of(chips)
    per_owner, rank, _ = ad.shape
    listed = rd.shape[0]
    half = x.shape[0] // chips // 2
    blocks = chips // 2
    run = max(1, blocks // 2)
    me = lax.axis_index("grp")
    sh = lax.axis_index("shard")
    chip, core = lax.div(sh, 2), lax.rem(sh, 2)
    other = 1 - core
    order = sorted(range(1, groups), key=lambda d: -min(d, groups - d))

    def hops(step):
        return min(step[0], high - step[0]) + min(step[1], across - step[1])

    steps = sorted(
        ((dy, dx) for dy in range(high) for dx in range(across)), key=lambda s: -hops(s)
    )
    row, column = lax.div(chip, across), lax.rem(chip, across)
    at_step = [
        lax.rem(row + dy, high) * across + lax.rem(column + dx, across) for dy, dx in steps
    ]

    def group_at(d):
        return lax.rem(me + d, groups)

    def send(src, dst, send_sem, recv_sem, to):
        pltpu.make_async_remote_copy(
            src_ref=src,
            dst_ref=dst,
            send_sem=send_sem,
            recv_sem=recv_sem,
            device_id=to,
            device_id_type=MESH,
        ).start()

    def all_bytes(ref, sem):
        pltpu.make_async_copy(ref, ref, sem).wait()

    tables = [
        pltpu.make_async_copy(src, dst, table_sem.at[i])
        for i, (src, dst) in enumerate(
            ((lists_hbm, lists), (slot_hbm, slot_of), (entry_hbm, entry_of), (rows_hbm, rows_of))
        )
    ]
    loads = [
        pltpu.make_async_copy(src, dst, load_sem.at[i])
        for i, (src, dst) in enumerate(
            ((ad_hbm, ad), (au_hbm, au), (x_hbm, x), (c_hbm, c), (rd_hbm, rd), (ru_hbm, ru))
        )
    ]
    tables[0].start()
    tables[1].start()
    loads[0].start()

    barrier = pltpu.get_barrier_semaphore()

    def greet(to):
        pl.semaphore_signal(barrier, inc=1, device_id=to, device_id_type=MESH)

    for d in order:
        greet((group_at(d), sh))
    for b in at_step[:-1]:
        greet((me, 2 * b + core))
    greet((me, 2 * chip + other))

    loads[1].start()
    tables[2].start()
    tables[3].start()
    for load in loads[2:]:
        load.start()

    tables[0].wait()
    tables[1].wait()
    firsts = []
    for d in range(groups):
        named = group_at(d)
        first, second = i32(-1), i32(-1)
        for e in range(listed):
            s = slot_of[lists[named, e]]
            mine = lax.div(s, i32(per_owner)) == me
            at = lax.rem(s, i32(per_owner))
            second = jnp.where(mine & (first >= 0), at, second)
            first = jnp.where(mine & (first < 0), at, first)
        slot_tab[2 * d] = first
        slot_tab[2 * d + 1] = second
        firsts.append((jnp.maximum(first, 0), jnp.maximum(second, 0)))

    def pack(own, out, into):
        for d in range(groups):
            for k in range(2):
                if d:
                    out[d - 1, k] = own[firsts[d][k]]
                else:
                    into[2 * me + k] = own[firsts[d][k]]

    def send_adapters(out, into, send_sem, recv_sem):
        for d in order:
            send(
                out.at[d - 1], into.at[pl.ds(2 * me, 2)], send_sem, recv_sem, (group_at(d), sh)
            )

    loads[0].wait()
    pack(ad, ad_out, ad_in)
    pl.semaphore_wait(barrier, groups - 1 + chips)
    send_adapters(ad_out, ad_in, ad_send, ad_recv)
    loads[1].wait()
    pack(au, au_out, au_in)
    all_bytes(ad_out, ad_send)
    send_adapters(au_out, au_in, au_send, au_recv)

    owners = [lax.div(slot_of[lists[me, e]], i32(per_owner)) for e in range(listed)]
    places = []
    for e in range(listed):
        k = i32(0)
        for before in range(e):
            k = k + jnp.where(owners[before] == owners[e], 1, 0)
        places.append(2 * owners[e] + k)
        place_tab[e] = places[e]
    for p in range(2 * groups):
        found = i32(0)
        for e in range(listed):
            found = jnp.where(places[e] == p, e, found)
        entry_tab[p] = found
    tables[2].wait()
    tables[3].wait()

    def project(tokens, adapters, mine, theirs, pair, which):
        def low_of(block, out, j):
            start = pl.multiple_of(block * 2 * half, 2 * half)
            low = lax.dot_general(
                adapters[place_tab[entry_of[block]]],
                tokens[pl.ds(start, 2 * half), :],
                (((1,), (1,)), ((), ())),
                preferred_element_type=f32,
            )
            out[2 * j] = low[:, :half]
            out[2 * j + 1] = low[:, half:]

        for first in range(0, blocks, run):
            for j in range(first, first + run):
                low_of(other * blocks + j, theirs, j)
            units = pl.ds(2 * first, 2 * run)
            send(
                theirs.at[units],
                pair.at[units],
                pair_send.at[which],
                pair_recv.at[which, first // run],
                (me, 2 * chip + other),
            )
        for j in range(blocks):
            low_of(core * blocks + j, mine, j)

    def scatter(mine, pair, rs, which):
        for first in range(0, blocks, run):
            units = pl.ds(2 * first, 2 * run)
            all_bytes(pair.at[units], pair_recv.at[which, first // run])
        mine[...] += pair[...]
        for i, q in enumerate(at_step[:-1]):
            send(mine.at[q], rs.at[i], rs_send.at[which], rs_recv.at[which], (me, 2 * q + core))

    def gather(mine, rs, ag, which):
        all_bytes(rs, rs_recv.at[which])
        low = mine[chip] + jnp.sum(rs[...], axis=0)
        token = lax.rem(chip, 2) * half + lax.broadcasted_iota(i32, (rank, half), 1)
        scale = jnp.where(token < rows_of[core * blocks + lax.div(chip, 2)], adapter_scale, 0.0)
        ag[core, chip] = (low * scale).astype(bf16)
        for b in at_step[:-1]:
            unit = ag.at[core, chip]
            send(unit, unit, ag_send.at[which], ag_recv.at[which], (me, 2 * b + core))

    def swap(ag, which):
        all_bytes(ag.at[core, pl.ds(0, chips - 1)], ag_recv.at[which])
        mine = ag.at[core]
        send(mine, mine, swap_send.at[which], swap_recv.at[which], (me, 2 * chip + other))

    def place(ag, h):
        for q in range(chips):
            e = entry_of[h * blocks + q // 2]
            v = ag[h, q]
            for l in range(listed):
                spread[h, l * rank : (l + 1) * rank, q * half : (q + 1) * half] = jnp.where(
                    e == l, v, jnp.zeros_like(v)
                )

    def product(tokens, h, start, stop):
        size = chips * half
        values = tokens[pl.ds(pl.multiple_of(h * size, size), size), start:stop]
        step = jnp.dot(spread[h], values, preferred_element_type=f32)
        return step.reshape(listed, rank, stop - start)

    def gradient_own(ag, tokens, residual, acc, cuts):
        place(ag, core)
        for start, stop in cuts:
            acc[:, :, start:stop] = residual[:, :, start:stop] + product(tokens, core, start, stop)

    def gradient_rest(ag, tokens, acc, which, cuts, ready):
        all_bytes(ag.at[other], swap_recv.at[which])
        place(ag, other)
        for start, stop in cuts:
            acc[:, :, start:stop] += product(tokens, other, start, stop)
            ready(start, stop)

    def send_gradient(acc, out, into, send_sem, recv_sem, start, stop):
        for d in order:
            owner = group_at(d)
            for k in range(2):
                out[d - 1, k, :, start:stop] = acc[entry_tab[2 * owner + k], :, start:stop].astype(
                    bf16
                )
            send(
                out.at[d - 1, :, :, start:stop],
                into.at[d - 1, :, :, start:stop],
                send_sem,
                recv_sem.at[d - 1],
                (owner, sh),
            )

    def collect(acc, into, recv, total):
        values = [acc[entry_tab[2 * me + k]] for k in range(2)]
        for s in range(per_owner):
            total[s] = jnp.where(slot_tab[0] == s, values[0], 0.0) + jnp.where(
                slot_tab[1] == s, values[1], 0.0
            )
        for d in reversed(order):
            all_bytes(into.at[d - 1], recv.at[d - 1])
            values = [into[d - 1, k].astype(f32) for k in range(2)]
            at = [slot_tab[2 * (groups - d) + k] for k in range(2)]
            for s in range(per_owner):
                total[s] += jnp.where(at[0] == s, values[0], 0.0) + jnp.where(
                    at[1] == s, values[1], 0.0
                )

    wd, wu = x.shape[1], c.shape[1]
    cut = wu // 2 // 256 * 256 + 256 if wu > 512 else wu
    cuts = [(s, e) for s, e in ((0, cut), (cut, wu)) if s < e]

    loads[2].wait()
    all_bytes(ad_in.at[pl.ds(0, 2 * groups - 2)], ad_recv)
    project(x, ad_in, mine_x, theirs_x, pair_x, 0)
    scatter(mine_x, pair_x, rs_x, 0)
    gather(mine_x, rs_x, ag_x, 0)

    loads[3].wait()
    all_bytes(au_in.at[pl.ds(0, 2 * groups - 2)], au_recv)
    project(c, au_in, mine_c, theirs_c, pair_c, 1)
    swap(ag_x, 0)
    scatter(mine_c, pair_c, rs_c, 1)

    loads[5].wait()
    gradient_own(ag_x, c, ru, acc_u, cuts)
    gradient_rest(
        ag_x,
        c,
        acc_u,
        0,
        cuts,
        functools.partial(send_gradient, acc_u, gu_out, gu_in, gu_send, gu_recv),
    )

    gather(mine_c, rs_c, ag_c, 1)
    swap(ag_c, 1)
    loads[4].wait()
    gradient_own(ag_c, x, rd, acc_d, [(0, wd)])
    gradient_rest(
        ag_c,
        x,
        acc_d,
        1,
        [(0, wd)],
        functools.partial(send_gradient, acc_d, gd_out, gd_in, gd_send, gd_recv),
    )

    collect(acc_u, gu_in, gu_recv, gu)
    collect(acc_d, gd_in, gd_recv, gd)

    all_bytes(au_out, au_send)
    for which, (pair, rs, ag) in enumerate(((pair_x, rs_x, ag_x), (pair_c, rs_c, ag_c))):
        all_bytes(pair, pair_send.at[which])
        all_bytes(rs, rs_send.at[which])
        all_bytes(ag.at[0, pl.ds(0, chips - 1)], ag_send.at[which])
        all_bytes(ag.at[0], swap_send.at[which])
    all_bytes(gu_out, gu_send)
    all_bytes(gd_out, gd_send)


def solution(mesh):
    groups, shards = mesh.shape["grp"], mesh.shape["shard"]

    def local(x, c, ad, au, rd, ru, lists, slot_of, entry_of, rows_of):
        tokens, wd = x.shape
        wu = c.shape[1]
        per_owner, rank, _ = ad.shape
        listed = lists.shape[1]
        chips = shards // 2
        half = tokens // chips // 2
        vmem, smem, dma = pltpu.VMEM, pltpu.SMEM, pltpu.SemaphoreType.DMA
        places = 2 * groups
        runs = chips // 2 // max(1, chips // 4)
        return pl.pallas_call(
            functools.partial(kernel, groups, shards),
            out_shape=(vmem((per_owner, rank, wd), f32), vmem((per_owner, rank, wu), f32)),
            in_specs=[pl.BlockSpec(memory_space=pltpu.HBM)] * 10,
            out_specs=[pl.BlockSpec(memory_space=pltpu.VMEM)] * 2,
            scratch_shapes=[
                vmem((tokens, wd), bf16),
                vmem((tokens, wu), bf16),
                vmem((per_owner, rank, wd), bf16),
                vmem((per_owner, rank, wu), bf16),
                vmem((listed, rank, wd), f32),
                vmem((listed, rank, wu), f32),
                vmem((groups - 1, 2, rank, wd), bf16),
                vmem((groups - 1, 2, rank, wu), bf16),
                vmem((places, rank, wd), bf16),
                vmem((places, rank, wu), bf16),
                vmem((chips, rank, half), f32),
                vmem((chips, rank, half), f32),
                vmem((chips, rank, half), f32),
                vmem((chips, rank, half), f32),
                vmem((chips, rank, half), f32),
                vmem((chips, rank, half), f32),
                vmem((chips - 1, rank, half), f32),
                vmem((chips - 1, rank, half), f32),
                vmem((2, chips, rank, half), bf16),
                vmem((2, chips, rank, half), bf16),
                vmem((2, listed * rank, chips * half), bf16),
                vmem((listed, rank, wd), f32),
                vmem((listed, rank, wu), f32),
                vmem((groups - 1, 2, rank, wd), bf16),
                vmem((groups - 1, 2, rank, wu), bf16),
                vmem((groups - 1, 2, rank, wd), bf16),
                vmem((groups - 1, 2, rank, wu), bf16),
                smem(lists.shape, i32),
                smem(slot_of.shape, i32),
                smem(entry_of.shape, i32),
                smem(rows_of.shape, i32),
                smem((places,), i32),
                smem((places,), i32),
                smem((listed,), i32),
                dma((6,)),
                dma((4,)),
                dma,
                dma,
                dma,
                dma,
                dma((2,)),
                dma((2, runs)),
                dma((2,)),
                dma((2,)),
                dma((2,)),
                dma((2,)),
                dma((2,)),
                dma((2,)),
                dma,
                dma((groups - 1,)),
                dma,
                dma((groups - 1,)),
            ],
            compiler_params=pltpu.CompilerParams(
                collective_id=0, has_side_effects=True, vmem_limit_bytes=56 * 2**20
            ),
        )(
            x,
            c,
            ad,
            au,
            rd,
            ru,
            lists,
            slot_of,
            entry_of,
            rows_of,
        )

    split = P("grp", None, "shard")
    return jax.shard_map(
        local,
        mesh=mesh,
        in_specs=(P("grp", "shard"),) * 2 + (split,) * 4 + (P(), P(), P("grp"), P("grp")),
        out_specs=(split, split),
        check_vma=False,
    )
```

```python
import functools

import jax
import jax.numpy as jnp
from jax import lax
from jax.experimental import pallas as pl
from jax.experimental.pallas import tpu as pltpu
from jax.sharding import PartitionSpec as P

MESH = pl.DeviceIdType.MESH
bf16, f32, i32 = jnp.bfloat16, jnp.float32, jnp.int32
adapter_scale = 2.0


def cuts_of(width):
    cut = (width // 2 // 256 + 1) * 256 if width > 512 else width // 2
    return [(0, cut), (cut, width)]


def grid_of(chips):
    across = 4 if chips % 4 == 0 else chips
    return chips // across, across


def kernel(
    groups,
    shards,
    x_hbm,
    c_hbm,
    ad_hbm,
    au_hbm,
    rd_hbm,
    ru_hbm,
    lists_hbm,
    slot_hbm,
    entry_hbm,
    rows_hbm,
    gd,
    gu,
    x,
    c,
    ad,
    au,
    rd,
    ru,
    ad_out,
    au_out,
    ad_in,
    au_in_0,
    au_in_1,
    mine_x,
    mine_c,
    theirs_x,
    theirs_c,
    pair_x,
    pair_c,
    rs_x,
    rs_c,
    ag_x,
    ag_c,
    spread,
    acc_d,
    acc_u,
    gd_out,
    gu_out,
    gd_in,
    gu_in,
    lists,
    slot_of,
    entry_of,
    rows_of,
    slot_tab,
    entry_tab,
    place_tab,
    load_sem,
    table_sem,
    ad_send,
    ad_recv,
    au_send,
    au_recv,
    pair_send,
    pair_recv,
    rs_send,
    rs_recv,
    ag_send,
    ag_recv,
    swap_send,
    swap_recv,
    gd_send,
    gd_recv,
    gu_send,
    gu_recv,
):
    chips = shards // 2
    high, across = grid_of(chips)
    per_owner, rank, _ = ad.shape
    listed = rd.shape[0]
    half = x.shape[0] // chips // 2
    blocks = chips // 2
    run = max(1, blocks // 2)
    me = lax.axis_index("grp")
    sh = lax.axis_index("shard")
    chip, core = lax.div(sh, 2), lax.rem(sh, 2)
    other = 1 - core
    order = sorted(range(1, groups), key=lambda d: -min(d, groups - d))
    wd, wu = x.shape[1], c.shape[1]
    cuts = cuts_of(wu)

    def hops(step):
        return min(step[0], high - step[0]) + min(step[1], across - step[1])

    steps = sorted(
        ((dy, dx) for dy in range(high) for dx in range(across)), key=lambda s: -hops(s)
    )
    row, column = lax.div(chip, across), lax.rem(chip, across)
    at_step = [
        lax.rem(row + dy, high) * across + lax.rem(column + dx, across) for dy, dx in steps
    ]

    def group_at(d):
        return lax.rem(me + d, groups)

    def send(src, dst, send_sem, recv_sem, to):
        pltpu.make_async_remote_copy(
            src_ref=src,
            dst_ref=dst,
            send_sem=send_sem,
            recv_sem=recv_sem,
            device_id=to,
            device_id_type=MESH,
        ).start()

    def all_bytes(ref, sem):
        pltpu.make_async_copy(ref, ref, sem).wait()

    tables = [
        pltpu.make_async_copy(src, dst, table_sem.at[i])
        for i, (src, dst) in enumerate(
            ((lists_hbm, lists), (slot_hbm, slot_of), (entry_hbm, entry_of), (rows_hbm, rows_of))
        )
    ]
    loads = [
        pltpu.make_async_copy(src, dst, load_sem.at[i])
        for i, (src, dst) in enumerate(
            ((ad_hbm, ad), (au_hbm, au), (x_hbm, x), (c_hbm, c), (rd_hbm, rd), (ru_hbm, ru))
        )
    ]
    tables[0].start()
    tables[1].start()
    loads[0].start()

    barrier = pltpu.get_barrier_semaphore()

    def greet(to):
        pl.semaphore_signal(barrier, inc=1, device_id=to, device_id_type=MESH)

    for d in order:
        greet((group_at(d), sh))
    for b in at_step[:-1]:
        greet((me, 2 * b + core))
    greet((me, 2 * chip + other))

    loads[1].start()
    tables[2].start()
    tables[3].start()

    tables[0].wait()
    tables[1].wait()
    firsts = []
    for d in range(groups):
        named = group_at(d)
        first, second = i32(-1), i32(-1)
        for e in range(listed):
            s = slot_of[lists[named, e]]
            mine = lax.div(s, i32(per_owner)) == me
            at = lax.rem(s, i32(per_owner))
            second = jnp.where(mine & (first >= 0), at, second)
            first = jnp.where(mine & (first < 0), at, first)
        slot_tab[2 * d] = first
        slot_tab[2 * d + 1] = second
        firsts.append((jnp.maximum(first, 0), jnp.maximum(second, 0)))

    def pack(own, out, parts):
        for d in range(groups):
            for k in range(2):
                if d:
                    out[d - 1, k] = own[firsts[d][k]]
                else:
                    for into, (start, stop) in parts:
                        into[2 * me + k] = own[firsts[d][k], :, start:stop]

    def send_adapters(out, into, send_sem, recv_sem, turns, start, stop):
        for d in turns:
            send(
                out.at[d - 1, :, :, start:stop],
                into.at[pl.ds(2 * me, 2)],
                send_sem,
                recv_sem,
                (group_at(d), sh),
            )

    loads[0].wait()
    pack(ad, ad_out, [(ad_in, (0, wd))])
    pl.semaphore_wait(barrier, groups - 1 + chips)
    send_adapters(ad_out, ad_in, ad_send, ad_recv, order, 0, wd)
    for load in loads[2:]:
        load.start()
    loads[1].wait()
    au_in = (au_in_0, au_in_1)
    pack(au, au_out, list(zip(au_in, cuts)))
    all_bytes(ad_out, ad_send)
    for i, (start, stop) in enumerate(cuts):
        send_adapters(au_out, au_in[i], au_send, au_recv.at[i], order, start, stop)

    owners = [lax.div(slot_of[lists[me, e]], i32(per_owner)) for e in range(listed)]
    places = []
    for e in range(listed):
        k = i32(0)
        for before in range(e):
            k = k + jnp.where(owners[before] == owners[e], 1, 0)
        places.append(2 * owners[e] + k)
        place_tab[e] = places[e]
    for p in range(2 * groups):
        found = i32(0)
        for e in range(listed):
            found = jnp.where(places[e] == p, e, found)
        entry_tab[p] = found
    tables[2].wait()
    tables[3].wait()

    def project(tokens, adapters, mine, theirs, pair, which, start, stop):
        def low_of(block, out, j):
            first = pl.multiple_of(block * 2 * half, 2 * half)
            low = lax.dot_general(
                adapters[place_tab[entry_of[block]]],
                tokens[pl.ds(first, 2 * half), start:stop],
                (((1,), (1,)), ((), ())),
                preferred_element_type=f32,
            )
            for h in range(2):
                value = low[:, h * half : (h + 1) * half]
                out[2 * j + h] = value if start == 0 else out[2 * j + h] + value

        for first in range(0, blocks, run):
            for j in range(first, first + run):
                low_of(other * blocks + j, theirs, j)
            if stop == tokens.shape[1]:
                units = pl.ds(2 * first, 2 * run)
                send(
                    theirs.at[units],
                    pair.at[units],
                    pair_send.at[which],
                    pair_recv.at[which, first // run],
                    (me, 2 * chip + other),
                )
        for j in range(blocks):
            low_of(core * blocks + j, mine, j)

    def scatter(mine, pair, rs, which):
        for first in range(0, blocks, run):
            units = pl.ds(2 * first, 2 * run)
            all_bytes(pair.at[units], pair_recv.at[which, first // run])
        mine[...] += pair[...]
        for i, q in enumerate(at_step[:-1]):
            send(mine.at[q], rs.at[i], rs_send.at[which], rs_recv.at[which], (me, 2 * q + core))

    def gather(mine, rs, ag, which):
        all_bytes(rs, rs_recv.at[which])
        low = mine[chip] + jnp.sum(rs[...], axis=0)
        token = lax.rem(chip, 2) * half + lax.broadcasted_iota(i32, (rank, half), 1)
        scale = jnp.where(token < rows_of[core * blocks + lax.div(chip, 2)], adapter_scale, 0.0)
        ag[core, chip] = (low * scale).astype(bf16)
        for b in at_step[:-1]:
            unit = ag.at[core, chip]
            send(unit, unit, ag_send.at[which], ag_recv.at[which], (me, 2 * b + core))

    def swap(ag, which):
        all_bytes(ag.at[core, pl.ds(0, chips - 1)], ag_recv.at[which])
        mine = ag.at[core]
        send(mine, mine, swap_send.at[which], swap_recv.at[which], (me, 2 * chip + other))

    def place(ag, h):
        for q in range(chips):
            e = entry_of[h * blocks + q // 2]
            v = ag[h, q]
            for l in range(listed):
                spread[h, l * rank : (l + 1) * rank, q * half : (q + 1) * half] = jnp.where(
                    e == l, v, jnp.zeros_like(v)
                )

    def product(tokens, h, start, stop):
        size = chips * half
        values = tokens[pl.ds(pl.multiple_of(h * size, size), size), start:stop]
        step = jnp.dot(spread[h], values, preferred_element_type=f32)
        return step.reshape(listed, rank, stop - start)

    def gradient_own(ag, tokens, residual, acc, cuts):
        place(ag, core)
        for start, stop in cuts:
            acc[:, :, start:stop] = residual[:, :, start:stop] + product(tokens, core, start, stop)

    def gradient_rest(tokens, acc, start, stop):
        acc[:, :, start:stop] += product(tokens, other, start, stop)

    def send_gradient(acc, out, into, send_sem, recv_sem, turns, start, stop):
        for d in turns:
            owner = group_at(d)
            for k in range(2):
                out[d - 1, k, :, start:stop] = acc[entry_tab[2 * owner + k], :, start:stop].astype(
                    bf16
                )
            send(
                out.at[d - 1, :, :, start:stop],
                into.at[d - 1, :, :, start:stop],
                send_sem,
                recv_sem.at[d - 1],
                (owner, sh),
            )

    def collect(acc, into, recv, total, turns):
        values = [acc[entry_tab[2 * me + k]] for k in range(2)]
        for s in range(per_owner):
            total[s] = jnp.where(slot_tab[0] == s, values[0], 0.0) + jnp.where(
                slot_tab[1] == s, values[1], 0.0
            )
        for d in reversed(turns):
            all_bytes(into.at[d - 1], recv.at[d - 1])
            values = [into[d - 1, k].astype(f32) for k in range(2)]
            at = [slot_tab[2 * (groups - d) + k] for k in range(2)]
            for s in range(per_owner):
                total[s] += jnp.where(at[0] == s, values[0], 0.0) + jnp.where(
                    at[1] == s, values[1], 0.0
                )

    arrived = pl.ds(0, 2 * groups - 2)
    loads[2].wait()
    all_bytes(ad_in.at[arrived], ad_recv)
    project(x, ad_in, mine_x, theirs_x, pair_x, 0, 0, wd)
    scatter(mine_x, pair_x, rs_x, 0)
    gather(mine_x, rs_x, ag_x, 0)

    loads[3].wait()
    loads[5].wait()
    for i, (start, stop) in enumerate(cuts):
        all_bytes(au_in[i].at[arrived], au_recv.at[i])
        project(c, au_in[i], mine_c, theirs_c, pair_c, 1, start, stop)
    scatter(mine_c, pair_c, rs_c, 1)

    swap(ag_x, 0)
    gradient_own(ag_x, c, ru, acc_u, cuts)
    all_bytes(ag_x.at[other], swap_recv.at[0])
    place(ag_x, other)
    for i, (start, stop) in enumerate(cuts):
        if i == len(cuts) - 1:
            gather(mine_c, rs_c, ag_c, 1)
        gradient_rest(c, acc_u, start, stop)
        send_gradient(acc_u, gu_out, gu_in, gu_send, gu_recv, order, start, stop)

    swap(ag_c, 1)
    loads[4].wait()
    gradient_own(ag_c, x, rd, acc_d, [(0, wd)])
    all_bytes(ag_c.at[other], swap_recv.at[1])
    place(ag_c, other)
    gradient_rest(x, acc_d, 0, wd)
    send_gradient(acc_d, gd_out, gd_in, gd_send, gd_recv, order, 0, wd)

    collect(acc_u, gu_in, gu_recv, gu, order)
    collect(acc_d, gd_in, gd_recv, gd, order)

    all_bytes(au_out, au_send)
    for which, (pair, rs, ag) in enumerate(((pair_x, rs_x, ag_x), (pair_c, rs_c, ag_c))):
        all_bytes(pair, pair_send.at[which])
        all_bytes(rs, rs_send.at[which])
        all_bytes(ag.at[0, pl.ds(0, chips - 1)], ag_send.at[which])
        all_bytes(ag.at[0], swap_send.at[which])
    all_bytes(gu_out, gu_send)
    all_bytes(gd_out, gd_send)


def solution(mesh):
    groups, shards = mesh.shape["grp"], mesh.shape["shard"]

    def local(x, c, ad, au, rd, ru, lists, slot_of, entry_of, rows_of):
        tokens, wd = x.shape
        wu = c.shape[1]
        per_owner, rank, _ = ad.shape
        listed = lists.shape[1]
        chips = shards // 2
        half = tokens // chips // 2
        vmem, smem, dma = pltpu.VMEM, pltpu.SMEM, pltpu.SemaphoreType.DMA
        places = 2 * groups
        runs = chips // 2 // max(1, chips // 4)
        return pl.pallas_call(
            functools.partial(kernel, groups, shards),
            out_shape=(vmem((per_owner, rank, wd), f32), vmem((per_owner, rank, wu), f32)),
            in_specs=[pl.BlockSpec(memory_space=pltpu.HBM)] * 10,
            out_specs=[pl.BlockSpec(memory_space=pltpu.VMEM)] * 2,
            scratch_shapes=[
                vmem((tokens, wd), bf16),
                vmem((tokens, wu), bf16),
                vmem((per_owner, rank, wd), bf16),
                vmem((per_owner, rank, wu), bf16),
                vmem((listed, rank, wd), f32),
                vmem((listed, rank, wu), f32),
                vmem((groups - 1, 2, rank, wd), bf16),
                vmem((groups - 1, 2, rank, wu), bf16),
                vmem((places, rank, wd), bf16),
                *(vmem((places, rank, stop - start), bf16) for start, stop in cuts_of(wu)),
                vmem((chips, rank, half), f32),
                vmem((chips, rank, half), f32),
                vmem((chips, rank, half), f32),
                vmem((chips, rank, half), f32),
                vmem((chips, rank, half), f32),
                vmem((chips, rank, half), f32),
                vmem((chips - 1, rank, half), f32),
                vmem((chips - 1, rank, half), f32),
                vmem((2, chips, rank, half), bf16),
                vmem((2, chips, rank, half), bf16),
                vmem((2, listed * rank, chips * half), bf16),
                vmem((listed, rank, wd), f32),
                vmem((listed, rank, wu), f32),
                vmem((groups - 1, 2, rank, wd), bf16),
                vmem((groups - 1, 2, rank, wu), bf16),
                vmem((groups - 1, 2, rank, wd), bf16),
                vmem((groups - 1, 2, rank, wu), bf16),
                smem(lists.shape, i32),
                smem(slot_of.shape, i32),
                smem(entry_of.shape, i32),
                smem(rows_of.shape, i32),
                smem((places,), i32),
                smem((places,), i32),
                smem((listed,), i32),
                dma((6,)),
                dma((4,)),
                dma,
                dma,
                dma,
                dma((2,)),
                dma((2,)),
                dma((2, runs)),
                dma((2,)),
                dma((2,)),
                dma((2,)),
                dma((2,)),
                dma((2,)),
                dma((2,)),
                dma,
                dma((groups - 1,)),
                dma,
                dma((groups - 1,)),
            ],
            compiler_params=pltpu.CompilerParams(
                collective_id=0, has_side_effects=True, vmem_limit_bytes=56 * 2**20
            ),
        )(
            x,
            c,
            ad,
            au,
            rd,
            ru,
            lists,
            slot_of,
            entry_of,
            rows_of,
        )

    split = P("grp", None, "shard")
    return jax.shard_map(
        local,
        mesh=mesh,
        in_specs=(P("grp", "shard"),) * 2 + (split,) * 4 + (P(), P(), P("grp"), P("grp")),
        out_specs=(split, split),
        check_vma=False,
    )
```

```python
import functools

import jax
import jax.numpy as jnp
from jax import lax
from jax.experimental import pallas as pl
from jax.experimental.pallas import tpu as pltpu
from jax.sharding import PartitionSpec as P

MESH = pl.DeviceIdType.MESH
bf16, f32, i32 = jnp.bfloat16, jnp.float32, jnp.int32
adapter_scale = 2.0


def cuts_of(width):
    cut = max(width - 256, 256)
    return [(0, cut), (cut, width)]


def grid_of(chips):
    across = 4 if chips % 4 == 0 else chips
    return chips // across, across


def kernel(
    groups,
    shards,
    x_hbm,
    c_hbm,
    ad_hbm,
    au_hbm,
    rd_hbm,
    ru_hbm,
    lists_hbm,
    slot_hbm,
    entry_hbm,
    rows_hbm,
    gd,
    gu,
    x,
    c,
    ad,
    au,
    rd,
    ru,
    ad_out,
    au_out,
    ad_in,
    au_in_0,
    au_in_1,
    mine_x,
    mine_c,
    theirs_x,
    theirs_c,
    pair_x,
    pair_c,
    rs_x,
    rs_c,
    ag_x,
    ag_c,
    spread,
    acc_d,
    acc_u,
    gd_out,
    gu_out,
    gd_in,
    gu_in,
    lists,
    slot_of,
    entry_of,
    rows_of,
    slot_tab,
    entry_tab,
    place_tab,
    load_sem,
    table_sem,
    ad_send,
    ad_recv,
    au_send,
    au_recv,
    pair_send,
    pair_recv,
    rs_send,
    rs_recv,
    ag_send,
    ag_recv,
    swap_send,
    swap_recv,
    gd_send,
    gd_recv,
    gu_send,
    gu_recv,
):
    chips = shards // 2
    high, across = grid_of(chips)
    per_owner, rank, _ = ad.shape
    listed = rd.shape[0]
    half = x.shape[0] // chips // 2
    blocks = chips // 2
    run = max(1, blocks // 2)
    me = lax.axis_index("grp")
    sh = lax.axis_index("shard")
    chip, core = lax.div(sh, 2), lax.rem(sh, 2)
    other = 1 - core
    order = sorted(range(1, groups), key=lambda d: -min(d, groups - d))
    wd, wu = x.shape[1], c.shape[1]
    cuts = cuts_of(wu)
    middle = (wu // 512 + 1) * 256
    halves = [(0, middle), (middle, wu)]

    def hops(step):
        return min(step[0], high - step[0]) + min(step[1], across - step[1])

    steps = sorted(
        ((dy, dx) for dy in range(high) for dx in range(across)), key=lambda s: -hops(s)
    )
    row, column = lax.div(chip, across), lax.rem(chip, across)
    at_step = [
        lax.rem(row + dy, high) * across + lax.rem(column + dx, across) for dy, dx in steps
    ]

    def group_at(d):
        return lax.rem(me + d, groups)

    def send(src, dst, send_sem, recv_sem, to):
        pltpu.make_async_remote_copy(
            src_ref=src,
            dst_ref=dst,
            send_sem=send_sem,
            recv_sem=recv_sem,
            device_id=to,
            device_id_type=MESH,
        ).start()

    def all_bytes(ref, sem):
        pltpu.make_async_copy(ref, ref, sem).wait()

    tables = [
        pltpu.make_async_copy(src, dst, table_sem.at[i])
        for i, (src, dst) in enumerate(
            ((lists_hbm, lists), (slot_hbm, slot_of), (entry_hbm, entry_of), (rows_hbm, rows_of))
        )
    ]
    loads = [
        pltpu.make_async_copy(src, dst, load_sem.at[i])
        for i, (src, dst) in enumerate(
            ((ad_hbm, ad), (au_hbm, au), (x_hbm, x), (c_hbm, c), (rd_hbm, rd), (ru_hbm, ru))
        )
    ]
    tables[0].start()
    tables[1].start()
    loads[0].start()

    barrier = pltpu.get_barrier_semaphore()

    def greet(to):
        pl.semaphore_signal(barrier, inc=1, device_id=to, device_id_type=MESH)

    for d in order:
        greet((group_at(d), sh))
    for b in at_step[:-1]:
        greet((me, 2 * b + core))
    greet((me, 2 * chip + other))

    loads[1].start()
    tables[2].start()
    tables[3].start()

    tables[0].wait()
    tables[1].wait()
    firsts = []
    for d in range(groups):
        named = group_at(d)
        first, second = i32(-1), i32(-1)
        for e in range(listed):
            s = slot_of[lists[named, e]]
            mine = lax.div(s, i32(per_owner)) == me
            at = lax.rem(s, i32(per_owner))
            second = jnp.where(mine & (first >= 0), at, second)
            first = jnp.where(mine & (first < 0), at, first)
        slot_tab[2 * d] = first
        slot_tab[2 * d + 1] = second
        firsts.append((jnp.maximum(first, 0), jnp.maximum(second, 0)))

    def pack(own, out, parts):
        for d in range(groups):
            for k in range(2):
                if d:
                    out[d - 1, k] = own[firsts[d][k]]
                else:
                    for into, (start, stop) in parts:
                        into[2 * me + k] = own[firsts[d][k], :, start:stop]

    def send_adapters(out, into, send_sem, recv_sem, start, stop, pieces):
        for k in range(0, 2, 2 // pieces):
            n = 2 // pieces
            for d in order:
                send(
                    out.at[d - 1, pl.ds(k, n), :, start:stop],
                    into.at[pl.ds(2 * me + k, n)],
                    send_sem,
                    recv_sem,
                    (group_at(d), sh),
                )

    loads[0].wait()
    pack(ad, ad_out, [(ad_in, (0, wd))])
    pl.semaphore_wait(barrier, groups - 1 + chips)
    send_adapters(ad_out, ad_in, ad_send, ad_recv, 0, wd, 1)
    for load in loads[2:]:
        load.start()
    loads[1].wait()
    au_in = (au_in_0, au_in_1)
    pack(au, au_out, list(zip(au_in, cuts)))
    all_bytes(ad_out, ad_send)
    for i, (start, stop) in enumerate(cuts):
        send_adapters(au_out, au_in[i], au_send, au_recv.at[i], start, stop, 2 - i)

    owners = [lax.div(slot_of[lists[me, e]], i32(per_owner)) for e in range(listed)]
    places = []
    for e in range(listed):
        k = i32(0)
        for before in range(e):
            k = k + jnp.where(owners[before] == owners[e], 1, 0)
        places.append(2 * owners[e] + k)
        place_tab[e] = places[e]
    for p in range(2 * groups):
        found = i32(0)
        for e in range(listed):
            found = jnp.where(places[e] == p, e, found)
        entry_tab[p] = found
    tables[2].wait()
    tables[3].wait()

    def project(tokens, adapters, mine, theirs, pair, which, start, stop):
        def low_of(block, out, j):
            first = pl.multiple_of(block * 2 * half, 2 * half)
            low = lax.dot_general(
                adapters[place_tab[entry_of[block]]],
                tokens[pl.ds(first, 2 * half), start:stop],
                (((1,), (1,)), ((), ())),
                preferred_element_type=f32,
            )
            for h in range(2):
                value = low[:, h * half : (h + 1) * half]
                out[2 * j + h] = value if start == 0 else out[2 * j + h] + value

        for first in range(0, blocks, run):
            for j in range(first, first + run):
                low_of(other * blocks + j, theirs, j)
            if stop == tokens.shape[1]:
                units = pl.ds(2 * first, 2 * run)
                send(
                    theirs.at[units],
                    pair.at[units],
                    pair_send.at[which],
                    pair_recv.at[which, first // run],
                    (me, 2 * chip + other),
                )
        for j in range(blocks):
            low_of(core * blocks + j, mine, j)

    def scatter(mine, pair, rs, which):
        for first in range(0, blocks, run):
            units = pl.ds(2 * first, 2 * run)
            all_bytes(pair.at[units], pair_recv.at[which, first // run])
        mine[...] += pair[...]
        for i, q in enumerate(at_step[:-1]):
            send(mine.at[q], rs.at[i], rs_send.at[which], rs_recv.at[which], (me, 2 * q + core))

    def gather(mine, rs, ag, which):
        all_bytes(rs, rs_recv.at[which])
        low = mine[chip] + jnp.sum(rs[...], axis=0)
        token = lax.rem(chip, 2) * half + lax.broadcasted_iota(i32, (rank, half), 1)
        scale = jnp.where(token < rows_of[core * blocks + lax.div(chip, 2)], adapter_scale, 0.0)
        ag[core, chip] = (low * scale).astype(bf16)
        for b in at_step[:-1]:
            unit = ag.at[core, chip]
            send(unit, unit, ag_send.at[which], ag_recv.at[which], (me, 2 * b + core))

    def swap(ag, which):
        all_bytes(ag.at[core, pl.ds(0, chips - 1)], ag_recv.at[which])
        mine = ag.at[core]
        send(mine, mine, swap_send.at[which], swap_recv.at[which], (me, 2 * chip + other))

    def place(ag, h):
        for q in range(chips):
            e = entry_of[h * blocks + q // 2]
            v = ag[h, q]
            for l in range(listed):
                spread[h, l * rank : (l + 1) * rank, q * half : (q + 1) * half] = jnp.where(
                    e == l, v, jnp.zeros_like(v)
                )

    def product(tokens, h, start, stop):
        size = chips * half
        values = tokens[pl.ds(pl.multiple_of(h * size, size), size), start:stop]
        step = jnp.dot(spread[h], values, preferred_element_type=f32)
        return step.reshape(listed, rank, stop - start)

    def gradient_own(ag, tokens, residual, acc, cuts):
        place(ag, core)
        for start, stop in cuts:
            acc[:, :, start:stop] = residual[:, :, start:stop] + product(tokens, core, start, stop)

    def gradient_rest(tokens, acc, start, stop):
        acc[:, :, start:stop] += product(tokens, other, start, stop)

    def send_gradient(acc, out, into, send_sem, recv_sem, turns, start, stop):
        for d in turns:
            owner = group_at(d)
            for k in range(2):
                out[d - 1, k, :, start:stop] = acc[entry_tab[2 * owner + k], :, start:stop].astype(
                    bf16
                )
            send(
                out.at[d - 1, :, :, start:stop],
                into.at[d - 1, :, :, start:stop],
                send_sem,
                recv_sem.at[d - 1],
                (owner, sh),
            )

    def collect(acc, into, recv, total, turns):
        values = [acc[entry_tab[2 * me + k]] for k in range(2)]
        for s in range(per_owner):
            total[s] = jnp.where(slot_tab[0] == s, values[0], 0.0) + jnp.where(
                slot_tab[1] == s, values[1], 0.0
            )
        for d in reversed(turns):
            all_bytes(into.at[d - 1], recv.at[d - 1])
            values = [into[d - 1, k].astype(f32) for k in range(2)]
            at = [slot_tab[2 * (groups - d) + k] for k in range(2)]
            for s in range(per_owner):
                total[s] += jnp.where(at[0] == s, values[0], 0.0) + jnp.where(
                    at[1] == s, values[1], 0.0
                )

    arrived = pl.ds(0, 2 * groups - 2)
    loads[2].wait()
    all_bytes(ad_in.at[arrived], ad_recv)
    project(x, ad_in, mine_x, theirs_x, pair_x, 0, 0, wd)
    scatter(mine_x, pair_x, rs_x, 0)
    gather(mine_x, rs_x, ag_x, 0)

    loads[3].wait()
    loads[5].wait()
    for i, (start, stop) in enumerate(cuts):
        all_bytes(au_in[i].at[arrived], au_recv.at[i])
        project(c, au_in[i], mine_c, theirs_c, pair_c, 1, start, stop)
    scatter(mine_c, pair_c, rs_c, 1)

    swap(ag_x, 0)
    gradient_own(ag_x, c, ru, acc_u, halves)
    all_bytes(ag_x.at[other], swap_recv.at[0])
    place(ag_x, other)
    for i, (start, stop) in enumerate(halves):
        if i == len(halves) - 1:
            gather(mine_c, rs_c, ag_c, 1)
        gradient_rest(c, acc_u, start, stop)
        send_gradient(acc_u, gu_out, gu_in, gu_send, gu_recv, order, start, stop)

    swap(ag_c, 1)
    loads[4].wait()
    gradient_own(ag_c, x, rd, acc_d, [(0, wd)])
    all_bytes(ag_c.at[other], swap_recv.at[1])
    place(ag_c, other)
    gradient_rest(x, acc_d, 0, wd)
    send_gradient(acc_d, gd_out, gd_in, gd_send, gd_recv, order, 0, wd)

    collect(acc_u, gu_in, gu_recv, gu, order)
    collect(acc_d, gd_in, gd_recv, gd, order)

    all_bytes(au_out, au_send)
    for which, (pair, rs, ag) in enumerate(((pair_x, rs_x, ag_x), (pair_c, rs_c, ag_c))):
        all_bytes(pair, pair_send.at[which])
        all_bytes(rs, rs_send.at[which])
        all_bytes(ag.at[0, pl.ds(0, chips - 1)], ag_send.at[which])
        all_bytes(ag.at[0], swap_send.at[which])
    all_bytes(gu_out, gu_send)
    all_bytes(gd_out, gd_send)


def solution(mesh):
    groups, shards = mesh.shape["grp"], mesh.shape["shard"]

    def local(x, c, ad, au, rd, ru, lists, slot_of, entry_of, rows_of):
        tokens, wd = x.shape
        wu = c.shape[1]
        per_owner, rank, _ = ad.shape
        listed = lists.shape[1]
        chips = shards // 2
        half = tokens // chips // 2
        vmem, smem, dma = pltpu.VMEM, pltpu.SMEM, pltpu.SemaphoreType.DMA
        places = 2 * groups
        runs = chips // 2 // max(1, chips // 4)
        return pl.pallas_call(
            functools.partial(kernel, groups, shards),
            out_shape=(vmem((per_owner, rank, wd), f32), vmem((per_owner, rank, wu), f32)),
            in_specs=[pl.BlockSpec(memory_space=pltpu.HBM)] * 10,
            out_specs=[pl.BlockSpec(memory_space=pltpu.VMEM)] * 2,
            scratch_shapes=[
                vmem((tokens, wd), bf16),
                vmem((tokens, wu), bf16),
                vmem((per_owner, rank, wd), bf16),
                vmem((per_owner, rank, wu), bf16),
                vmem((listed, rank, wd), f32),
                vmem((listed, rank, wu), f32),
                vmem((groups - 1, 2, rank, wd), bf16),
                vmem((groups - 1, 2, rank, wu), bf16),
                vmem((places, rank, wd), bf16),
                *(vmem((places, rank, stop - start), bf16) for start, stop in cuts_of(wu)),
                vmem((chips, rank, half), f32),
                vmem((chips, rank, half), f32),
                vmem((chips, rank, half), f32),
                vmem((chips, rank, half), f32),
                vmem((chips, rank, half), f32),
                vmem((chips, rank, half), f32),
                vmem((chips - 1, rank, half), f32),
                vmem((chips - 1, rank, half), f32),
                vmem((2, chips, rank, half), bf16),
                vmem((2, chips, rank, half), bf16),
                vmem((2, listed * rank, chips * half), bf16),
                vmem((listed, rank, wd), f32),
                vmem((listed, rank, wu), f32),
                vmem((groups - 1, 2, rank, wd), bf16),
                vmem((groups - 1, 2, rank, wu), bf16),
                vmem((groups - 1, 2, rank, wd), bf16),
                vmem((groups - 1, 2, rank, wu), bf16),
                smem(lists.shape, i32),
                smem(slot_of.shape, i32),
                smem(entry_of.shape, i32),
                smem(rows_of.shape, i32),
                smem((places,), i32),
                smem((places,), i32),
                smem((listed,), i32),
                dma((6,)),
                dma((4,)),
                dma,
                dma,
                dma,
                dma((2,)),
                dma((2,)),
                dma((2, runs)),
                dma((2,)),
                dma((2,)),
                dma((2,)),
                dma((2,)),
                dma((2,)),
                dma((2,)),
                dma,
                dma((groups - 1,)),
                dma,
                dma((groups - 1,)),
            ],
            compiler_params=pltpu.CompilerParams(
                collective_id=0, has_side_effects=True, vmem_limit_bytes=56 * 2**20
            ),
        )(
            x,
            c,
            ad,
            au,
            rd,
            ru,
            lists,
            slot_of,
            entry_of,
            rows_of,
        )

    split = P("grp", None, "shard")
    return jax.shard_map(
        local,
        mesh=mesh,
        in_specs=(P("grp", "shard"),) * 2 + (split,) * 4 + (P(), P(), P("grp"), P("grp")),
        out_specs=(split, split),
        check_vma=False,
    )
```

```python
import functools

import jax
import jax.numpy as jnp
from jax import lax
from jax.experimental import pallas as pl
from jax.experimental.pallas import tpu as pltpu
from jax.sharding import PartitionSpec as P

MESH = pl.DeviceIdType.MESH
bf16, f32, i32 = jnp.bfloat16, jnp.float32, jnp.int32
adapter_scale = 2.0


def cuts_of(width):
    cut = max(width - 256, 256)
    return [(0, cut), (cut, width)]


def grid_of(chips):
    across = 4 if chips % 4 == 0 else chips
    return chips // across, across


def kernel(
    groups,
    shards,
    x_hbm,
    c_hbm,
    ad_hbm,
    au_hbm,
    rd_hbm,
    ru_hbm,
    lists_hbm,
    slot_hbm,
    entry_hbm,
    rows_hbm,
    gd,
    gu,
    x,
    c,
    ad,
    au,
    rd,
    ru,
    ad_out,
    au_out,
    ad_in,
    au_in_0,
    au_in_1,
    mine_x,
    mine_c,
    theirs_x,
    theirs_c,
    pair_x,
    pair_c,
    rs_x,
    rs_c,
    ag_x,
    ag_c,
    spread,
    acc_d,
    acc_u,
    gd_out,
    gu_out,
    gd_in,
    gu_in,
    lists,
    slot_of,
    entry_of,
    rows_of,
    slot_tab,
    entry_tab,
    place_tab,
    load_sem,
    table_sem,
    ad_send,
    ad_recv,
    au_send,
    au_recv,
    pair_send,
    pair_recv,
    rs_send,
    rs_recv,
    ag_send,
    ag_recv,
    swap_send,
    swap_recv,
    gd_send,
    gd_recv,
    gu_send,
    gu_recv,
):
    chips = shards // 2
    high, across = grid_of(chips)
    per_owner, rank, _ = ad.shape
    listed = rd.shape[0]
    half = x.shape[0] // chips // 2
    blocks = chips // 2
    run = max(1, blocks // 2)
    me = lax.axis_index("grp")
    sh = lax.axis_index("shard")
    chip, core = lax.div(sh, 2), lax.rem(sh, 2)
    other = 1 - core
    order = sorted(range(1, groups), key=lambda d: -min(d, groups - d))
    wd, wu = x.shape[1], c.shape[1]
    cuts = cuts_of(wu)
    middle = (wu // 512 + 1) * 256
    halves = [(0, middle), (middle, wu)]

    def hops(step):
        return min(step[0], high - step[0]) + min(step[1], across - step[1])

    steps = sorted(
        ((dy, dx) for dy in range(high) for dx in range(across)), key=lambda s: -hops(s)
    )
    row, column = lax.div(chip, across), lax.rem(chip, across)
    at_step = [
        lax.rem(row + dy, high) * across + lax.rem(column + dx, across) for dy, dx in steps
    ]

    def group_at(d):
        return lax.rem(me + d, groups)

    def send(src, dst, send_sem, recv_sem, to):
        pltpu.make_async_remote_copy(
            src_ref=src,
            dst_ref=dst,
            send_sem=send_sem,
            recv_sem=recv_sem,
            device_id=to,
            device_id_type=MESH,
        ).start()

    def all_bytes(ref, sem):
        pltpu.make_async_copy(ref, ref, sem).wait()

    tables = [
        pltpu.make_async_copy(src, dst, table_sem.at[i])
        for i, (src, dst) in enumerate(
            ((lists_hbm, lists), (slot_hbm, slot_of), (entry_hbm, entry_of), (rows_hbm, rows_of))
        )
    ]
    loads = [
        pltpu.make_async_copy(src, dst, load_sem.at[i])
        for i, (src, dst) in enumerate(
            ((ad_hbm, ad), (au_hbm, au), (x_hbm, x), (c_hbm, c), (rd_hbm, rd), (ru_hbm, ru))
        )
    ]
    barrier = pltpu.get_barrier_semaphore()

    def greet(to):
        pl.semaphore_signal(barrier, inc=1, device_id=to, device_id_type=MESH)

    for d in order:
        greet((group_at(d), sh))
    for b in at_step[:-1]:
        greet((me, 2 * b + core))
    greet((me, 2 * chip + other))

    tables[0].start()
    tables[1].start()
    loads[0].start()
    loads[1].start()
    tables[2].start()
    tables[3].start()

    tables[0].wait()
    tables[1].wait()
    firsts = []
    for d in range(groups):
        named = group_at(d)
        first, second = i32(-1), i32(-1)
        for e in range(listed):
            s = slot_of[lists[named, e]]
            mine = lax.div(s, i32(per_owner)) == me
            at = lax.rem(s, i32(per_owner))
            second = jnp.where(mine & (first >= 0), at, second)
            first = jnp.where(mine & (first < 0), at, first)
        slot_tab[2 * d] = first
        slot_tab[2 * d + 1] = second
        firsts.append((jnp.maximum(first, 0), jnp.maximum(second, 0)))

    def pack(own, out, parts):
        for d in range(groups):
            for k in range(2):
                if d:
                    out[d - 1, k] = own[firsts[d][k]]
                else:
                    for into, (start, stop) in parts:
                        into[2 * me + k] = own[firsts[d][k], :, start:stop]

    def send_adapters(out, into, send_sem, recv_sem, start, stop, pieces):
        for k in range(0, 2, 2 // pieces):
            n = 2 // pieces
            for d in order:
                send(
                    out.at[d - 1, pl.ds(k, n), :, start:stop],
                    into.at[pl.ds(2 * me + k, n)],
                    send_sem,
                    recv_sem,
                    (group_at(d), sh),
                )

    loads[0].wait()
    pack(ad, ad_out, [(ad_in, (0, wd))])
    pl.semaphore_wait(barrier, groups - 1 + chips)
    send_adapters(ad_out, ad_in, ad_send, ad_recv, 0, wd, 1)
    for load in loads[2:]:
        load.start()
    loads[1].wait()
    au_in = (au_in_0, au_in_1)
    pack(au, au_out, list(zip(au_in, cuts)))
    all_bytes(ad_out, ad_send)
    for i, (start, stop) in enumerate(cuts):
        send_adapters(au_out, au_in[i], au_send, au_recv.at[i], start, stop, 2 - i)

    owners = [lax.div(slot_of[lists[me, e]], i32(per_owner)) for e in range(listed)]
    places = []
    for e in range(listed):
        k = i32(0)
        for before in range(e):
            k = k + jnp.where(owners[before] == owners[e], 1, 0)
        places.append(2 * owners[e] + k)
        place_tab[e] = places[e]
    for p in range(2 * groups):
        found = i32(0)
        for e in range(listed):
            found = jnp.where(places[e] == p, e, found)
        entry_tab[p] = found
    tables[2].wait()
    tables[3].wait()

    def project(tokens, adapters, mine, theirs, pair, which, start, stop):
        def low_of(block, out, j):
            first = pl.multiple_of(block * 2 * half, 2 * half)
            low = lax.dot_general(
                adapters[place_tab[entry_of[block]]],
                tokens[pl.ds(first, 2 * half), start:stop],
                (((1,), (1,)), ((), ())),
                preferred_element_type=f32,
            )
            for h in range(2):
                value = low[:, h * half : (h + 1) * half]
                out[2 * j + h] = value if start == 0 else out[2 * j + h] + value

        for first in range(0, blocks, run):
            for j in range(first, first + run):
                low_of(other * blocks + j, theirs, j)
            if stop == tokens.shape[1]:
                units = pl.ds(2 * first, 2 * run)
                send(
                    theirs.at[units],
                    pair.at[units],
                    pair_send.at[which],
                    pair_recv.at[which, first // run],
                    (me, 2 * chip + other),
                )
        for j in range(blocks):
            low_of(core * blocks + j, mine, j)

    def scatter(mine, pair, rs, which):
        for first in range(0, blocks, run):
            units = pl.ds(2 * first, 2 * run)
            all_bytes(pair.at[units], pair_recv.at[which, first // run])
        mine[...] += pair[...]
        for i, q in enumerate(at_step[:-1]):
            send(mine.at[q], rs.at[i], rs_send.at[which], rs_recv.at[which], (me, 2 * q + core))

    def gather(mine, rs, ag, which):
        all_bytes(rs, rs_recv.at[which])
        low = mine[chip] + jnp.sum(rs[...], axis=0)
        token = lax.rem(chip, 2) * half + lax.broadcasted_iota(i32, (rank, half), 1)
        scale = jnp.where(token < rows_of[core * blocks + lax.div(chip, 2)], adapter_scale, 0.0)
        ag[core, chip] = (low * scale).astype(bf16)
        for b in at_step[:-1]:
            unit = ag.at[core, chip]
            send(unit, unit, ag_send.at[which], ag_recv.at[which], (me, 2 * b + core))

    def swap(ag, which):
        all_bytes(ag.at[core, pl.ds(0, chips - 1)], ag_recv.at[which])
        mine = ag.at[core]
        send(mine, mine, swap_send.at[which], swap_recv.at[which], (me, 2 * chip + other))

    def place(ag, h):
        for q in range(chips):
            e = entry_of[h * blocks + q // 2]
            v = ag[h, q]
            for l in range(listed):
                spread[h, l * rank : (l + 1) * rank, q * half : (q + 1) * half] = jnp.where(
                    e == l, v, jnp.zeros_like(v)
                )

    def product(tokens, h, start, stop):
        size = chips * half
        values = tokens[pl.ds(pl.multiple_of(h * size, size), size), start:stop]
        step = jnp.dot(spread[h], values, preferred_element_type=f32)
        return step.reshape(listed, rank, stop - start)

    def gradient_own(ag, tokens, residual, acc, cuts):
        place(ag, core)
        for start, stop in cuts:
            acc[:, :, start:stop] = residual[:, :, start:stop] + product(tokens, core, start, stop)

    def gradient_rest(tokens, acc, start, stop):
        acc[:, :, start:stop] += product(tokens, other, start, stop)

    def send_gradient(acc, out, into, send_sem, recv_sem, turns, start, stop):
        for d in turns:
            owner = group_at(d)
            for k in range(2):
                out[d - 1, k, :, start:stop] = acc[entry_tab[2 * owner + k], :, start:stop].astype(
                    bf16
                )
            send(
                out.at[d - 1, :, :, start:stop],
                into.at[d - 1, :, :, start:stop],
                send_sem,
                recv_sem.at[d - 1],
                (owner, sh),
            )

    def collect(acc, into, recv, total, turns):
        values = [acc[entry_tab[2 * me + k]] for k in range(2)]
        for s in range(per_owner):
            total[s] = jnp.where(slot_tab[0] == s, values[0], 0.0) + jnp.where(
                slot_tab[1] == s, values[1], 0.0
            )
        for d in reversed(turns):
            all_bytes(into.at[d - 1], recv.at[d - 1])
            values = [into[d - 1, k].astype(f32) for k in range(2)]
            at = [slot_tab[2 * (groups - d) + k] for k in range(2)]
            for s in range(per_owner):
                total[s] += jnp.where(at[0] == s, values[0], 0.0) + jnp.where(
                    at[1] == s, values[1], 0.0
                )

    arrived = pl.ds(0, 2 * groups - 2)
    loads[2].wait()
    all_bytes(ad_in.at[arrived], ad_recv)
    project(x, ad_in, mine_x, theirs_x, pair_x, 0, 0, wd)
    scatter(mine_x, pair_x, rs_x, 0)
    gather(mine_x, rs_x, ag_x, 0)

    loads[3].wait()
    loads[5].wait()
    for i, (start, stop) in enumerate(cuts):
        all_bytes(au_in[i].at[arrived], au_recv.at[i])
        project(c, au_in[i], mine_c, theirs_c, pair_c, 1, start, stop)
    scatter(mine_c, pair_c, rs_c, 1)

    swap(ag_x, 0)
    gradient_own(ag_x, c, ru, acc_u, halves)
    all_bytes(ag_x.at[other], swap_recv.at[0])
    place(ag_x, other)
    for i, (start, stop) in enumerate(halves):
        if i == len(halves) - 1:
            gather(mine_c, rs_c, ag_c, 1)
        gradient_rest(c, acc_u, start, stop)
        send_gradient(acc_u, gu_out, gu_in, gu_send, gu_recv, order, start, stop)

    swap(ag_c, 1)
    loads[4].wait()
    gradient_own(ag_c, x, rd, acc_d, [(0, wd)])
    all_bytes(ag_c.at[other], swap_recv.at[1])
    place(ag_c, other)
    gradient_rest(x, acc_d, 0, wd)
    send_gradient(acc_d, gd_out, gd_in, gd_send, gd_recv, order, 0, wd)

    collect(acc_u, gu_in, gu_recv, gu, order)
    collect(acc_d, gd_in, gd_recv, gd, order)

    all_bytes(au_out, au_send)
    for which, (pair, rs, ag) in enumerate(((pair_x, rs_x, ag_x), (pair_c, rs_c, ag_c))):
        all_bytes(pair, pair_send.at[which])
        all_bytes(rs, rs_send.at[which])
        all_bytes(ag.at[0, pl.ds(0, chips - 1)], ag_send.at[which])
        all_bytes(ag.at[0], swap_send.at[which])
    all_bytes(gu_out, gu_send)
    all_bytes(gd_out, gd_send)


def solution(mesh):
    groups, shards = mesh.shape["grp"], mesh.shape["shard"]

    def local(x, c, ad, au, rd, ru, lists, slot_of, entry_of, rows_of):
        tokens, wd = x.shape
        wu = c.shape[1]
        per_owner, rank, _ = ad.shape
        listed = lists.shape[1]
        chips = shards // 2
        half = tokens // chips // 2
        vmem, smem, dma = pltpu.VMEM, pltpu.SMEM, pltpu.SemaphoreType.DMA
        places = 2 * groups
        runs = chips // 2 // max(1, chips // 4)
        return pl.pallas_call(
            functools.partial(kernel, groups, shards),
            out_shape=(vmem((per_owner, rank, wd), f32), vmem((per_owner, rank, wu), f32)),
            in_specs=[pl.BlockSpec(memory_space=pltpu.HBM)] * 10,
            out_specs=[pl.BlockSpec(memory_space=pltpu.VMEM)] * 2,
            scratch_shapes=[
                vmem((tokens, wd), bf16),
                vmem((tokens, wu), bf16),
                vmem((per_owner, rank, wd), bf16),
                vmem((per_owner, rank, wu), bf16),
                vmem((listed, rank, wd), f32),
                vmem((listed, rank, wu), f32),
                vmem((groups - 1, 2, rank, wd), bf16),
                vmem((groups - 1, 2, rank, wu), bf16),
                vmem((places, rank, wd), bf16),
                *(vmem((places, rank, stop - start), bf16) for start, stop in cuts_of(wu)),
                vmem((chips, rank, half), f32),
                vmem((chips, rank, half), f32),
                vmem((chips, rank, half), f32),
                vmem((chips, rank, half), f32),
                vmem((chips, rank, half), f32),
                vmem((chips, rank, half), f32),
                vmem((chips - 1, rank, half), f32),
                vmem((chips - 1, rank, half), f32),
                vmem((2, chips, rank, half), bf16),
                vmem((2, chips, rank, half), bf16),
                vmem((2, listed * rank, chips * half), bf16),
                vmem((listed, rank, wd), f32),
                vmem((listed, rank, wu), f32),
                vmem((groups - 1, 2, rank, wd), bf16),
                vmem((groups - 1, 2, rank, wu), bf16),
                vmem((groups - 1, 2, rank, wd), bf16),
                vmem((groups - 1, 2, rank, wu), bf16),
                smem(lists.shape, i32),
                smem(slot_of.shape, i32),
                smem(entry_of.shape, i32),
                smem(rows_of.shape, i32),
                smem((places,), i32),
                smem((places,), i32),
                smem((listed,), i32),
                dma((6,)),
                dma((4,)),
                dma,
                dma,
                dma,
                dma((2,)),
                dma((2,)),
                dma((2, runs)),
                dma((2,)),
                dma((2,)),
                dma((2,)),
                dma((2,)),
                dma((2,)),
                dma((2,)),
                dma,
                dma((groups - 1,)),
                dma,
                dma((groups - 1,)),
            ],
            compiler_params=pltpu.CompilerParams(
                collective_id=0, has_side_effects=True, vmem_limit_bytes=56 * 2**20
            ),
        )(
            x,
            c,
            ad,
            au,
            rd,
            ru,
            lists,
            slot_of,
            entry_of,
            rows_of,
        )

    split = P("grp", None, "shard")
    return jax.shard_map(
        local,
        mesh=mesh,
        in_specs=(P("grp", "shard"),) * 2 + (split,) * 4 + (P(), P(), P("grp"), P("grp")),
        out_specs=(split, split),
        check_vma=False,
    )
```
